256 devices in a mesh: section: 16 (over z, core), sp: 16 (over x, y).
Axes of the slice: x: 4, y: 4, z: 8, core: 2. Of those that a mesh axis runs over, the one named last changes fastest.
Arguments:
- activations: bfloat16 [16, 512, 3072], P('section', 'sp'), may hold values from -6 to 6
- modulation: float32 [16, 3, 3072], P('section'), may hold values from -3 to 3
- w_qkv: bfloat16 [16, 3072, 3, 2048], P('section', None, None, 'sp'), may hold values from -0.15625 to 0.15625
- w_mlp_in: bfloat16 [16, 3072, 6144], P('section', None, 'sp'), may hold values from -0.109375 to 0.109375
- w_out_attn: bfloat16 [16, 2048, 3072], P('section', 'sp'), may hold values from -0.125 to 0.125
- w_out_mlp: bfloat16 [16, 6144, 3072], P('section', 'sp'), may hold values from -0.078125 to 0.078125
- key_cache: bfloat16 [16, 6144, 2048], P('section', None, 'sp'), may hold values from -100 to 100
- value_cache: bfloat16 [16, 6144, 2048], P('section', None, 'sp'), may hold values from -8 to 8
- patch_order: int32 [16], replicated, may hold values from 0 to 15
- patch_lengths: int32 [16], replicated, may hold values from 1 to 512, 6144 in all
Outputs:
- section_output: float32 [16, 512, 3072], P('section', 'sp')
The draws below stay inside these ranges and needn't reach their ends.
Inputs may be any that keep to these rules, and one draw needn't show every extreme that they name: `patch_lengths`: the lengths sum to 6144 and the largest is 512.
All inputs are finite; a program needn't handle non-finite values.
Results may differ from the reference program's by a relative error of at most 0.03.
Values may be sent and summed in bfloat16 or wider, within the bound.
No kernel may reach another device: no remote copies, remote signals or barrier semaphores. Data moves between devices by JAX's collectives and lax.ppermute only.
A program may use at most 128 MiB of HBM per device.

```python
import math
import jax
import jax.numpy as jnp
import numpy as np
from jax import lax

D = 3072
HEADS = 16
HD = 128
FF = 6144
PATCHES = 16
TICKS = 2
PMAX = 512
SEQ = 6144
N_SECTION = 16


def draw_key_cache(key, part):
    key = jax.random.fold_in(key, 7)
    base_key = jax.random.fold_in(key, 0)
    full_shape = (N_SECTION, SEQ, HEADS * HD)
    entries = jnp.clip(1.4 * jax.random.normal(base_key, full_shape, jnp.float32), -8.4, 8.4)
    return entries.astype(jnp.bfloat16)


def with_ends(drawn, stream_key, smallest, high):
    shape = drawn.shape
    index_at = [jax.random.randint(jax.random.fold_in(stream_key, axis), (), 0, shape[axis]) for axis in range(len(shape))]
    drawn = drawn.at[tuple(index_at)].set(smallest)
    longest = shape.index(max(shape))
    index_at[longest] = (index_at[longest] + 1) % shape[longest]
    return drawn.at[tuple(index_at)].set(high)


def block_levels(rng, shape, shards, low, high):
    def one(dim, blocks):
        heights = jax.random.uniform(jax.random.fold_in(jax.random.fold_in(rng, 6), dim), (blocks,), jnp.float32, low / len(shards), high / len(shards))
        return jnp.repeat(jnp.exp(heights), shape[dim] // blocks).reshape((-1,) + (1,) * (len(shape) - dim - 1))

    factor_of = one(*shards[0])
    for cut in shards[1:]:
        factor_of = factor_of * one(*cut)
    return factor_of


def length_profile(count, total, reach, skew):
    portions = [(1 << 20) // math.isqrt(grade ** skew) + 1 for grade in range(2, count + 1)]
    spare, counts = total - reach - (count - 1), [1] * (count - 1)
    while spare > 0:
        candidates = [i for i in range(count - 1) if counts[i] < reach]
        whole, remaining = sum([portions[i] for i in candidates]), spare
        for i in candidates:
            addition = min(reach - counts[i], max(1, remaining * portions[i] // whole), spare)
            counts[i] = counts[i] + addition
            spare = spare - addition
    return np.array([reach] + counts)


def ragged_sizes(key, count, total, reach, lean):
    if count == 2:
        one = jax.random.randint(key, (), max(1, total - reach), min(reach, total - 1) + 1)
        return jnp.stack([one, total - one])
    tallies = jnp.asarray(length_profile(count, total, reach, lean), jnp.int32)
    twos = (count - 1) // 2
    source_of, taker = tallies[1:1 + 2 * twos:2], tallies[2:2 + 2 * twos:2]
    margin = jnp.minimum(source_of - 1, reach - taker)
    moved = jax.random.randint(jax.random.fold_in(key, 1), (twos,), 0, 1 << 20) % (margin + 1)
    tallies = tallies.at[1:1 + 2 * twos:2].set(source_of - moved).at[2:2 + 2 * twos:2].set(taker + moved)
    return tallies[jax.random.permutation(jax.random.fold_in(key, 2), count)]


def centred(stream_key, shape, scale, bound, cuts=(), kind=jnp.bfloat16):
    values = scale * jax.random.normal(stream_key, shape, jnp.float32)
    if cuts:
        values = values * block_levels(stream_key, shape, cuts, -0.22, 0.18)
    return jnp.clip(values, -bound, bound).astype(kind)


def setup_inputs(seed: int = 0) -> dict:
    seeds = jax.random.split(jax.random.key(seed), 11)
    return {
        "activations": centred(seeds[0], (N_SECTION, PMAX, D), 1.0, 6.0, ((0, 16), (1, 16))),
        "modulation": centred(seeds[1], (N_SECTION, 3, D), 0.5, 3.0, ((0, 16),), jnp.float32),
        "w_qkv": centred(seeds[2], (N_SECTION, D, 3, HEADS * HD), (D // 2) ** -0.5, 0.15625, ((0, 16), (3, 16))),
        "w_mlp_in": centred(seeds[3], (N_SECTION, D, FF), D ** -0.5, 0.109375, ((0, 16), (2, 16))),
        "w_out_attn": centred(seeds[4], (N_SECTION, HEADS * HD, D), (HEADS * HD) ** -0.5, 0.125, ((0, 16), (1, 16))),
        "w_out_mlp": centred(seeds[5], (N_SECTION, FF, D), FF ** -0.5, 0.078125, ((0, 16), (1, 16))),
        "key_cache": draw_key_cache(jax.random.fold_in(seeds[10], 71), 0),
        "value_cache": centred(seeds[7], (N_SECTION, SEQ, HEADS * HD), 1.4, 8.0, ((0, 16), (2, 16))),
        "patch_order": with_ends(jax.random.randint(seeds[8], (N_SECTION,), 0, PATCHES), jax.random.fold_in(seeds[8], 1), 0, PATCHES - 1).astype(jnp.int32),
        "patch_lengths": ragged_sizes(seeds[9], PATCHES, SEQ, PMAX, 0).astype(jnp.int32),
    }


norm_eps = 1e-06

def modulate(current, shift_vec, scale_vec):
    values = current.astype(jnp.float32)
    row_mean = lax.optimization_barrier(jnp.mean(values, axis=-1, keepdims=True))
    centered = values - row_mean
    row_var = lax.optimization_barrier(jnp.mean(centered * centered, axis=-1, keepdims=True))
    normed = centered * lax.rsqrt(row_var + norm_eps)
    return (normed * (1.0 + scale_vec) + shift_vec).astype(jnp.bfloat16)

def place_rows(cache_rows, fresh_rows, first_row, patch_len):
    slot_count = fresh_rows.shape[0]
    padded_cache = jnp.concatenate([cache_rows, jnp.zeros((slot_count, cache_rows.shape[1]), cache_rows.dtype)], axis=0)
    old_window = lax.dynamic_slice_in_dim(padded_cache, first_row, slot_count, 0)
    valid_rows = (jnp.arange(slot_count, dtype=jnp.int32) < patch_len)[:, None]
    padded_cache = lax.dynamic_update_slice_in_dim(padded_cache, jnp.where(valid_rows, fresh_rows, old_window), first_row, 0)
    return padded_cache[:cache_rows.shape[0]]

def attend(queries, keys_all, values_all):
    slot_count, head_cols = queries.shape
    head_count = head_cols // HD
    q_heads = queries.reshape(slot_count, head_count, HD).astype(jnp.float32)
    k_heads = keys_all.reshape(keys_all.shape[0], head_count, HD).astype(jnp.float32)
    v_heads = values_all.reshape(values_all.shape[0], head_count, HD).astype(jnp.float32)
    scores = jnp.einsum('qhd,khd->hqk', q_heads, k_heads, precision=lax.Precision.HIGHEST) * (1.0 / math.sqrt(HD))
    attn_probs = jax.nn.softmax(scores, axis=-1).astype(jnp.bfloat16)
    attended = jnp.einsum('hqk,khd->qhd', attn_probs.astype(jnp.float32), v_heads)
    return attended.reshape(slot_count, head_cols).astype(jnp.bfloat16)

def section_block(section_items):
    current, modulation, w_qkv, w_mlp_in, w_out_attn, w_out_mlp, key_cache, value_cache, first_row, patch_len = section_items
    modulated = modulate(current, modulation[0], modulation[1])
    head_cols = w_qkv.shape[2]
    projected = jnp.dot(modulated, w_qkv.reshape(w_qkv.shape[0], 3 * head_cols), preferred_element_type=jnp.float32)
    queries = projected[:, :head_cols]
    fresh_keys = projected[:, head_cols:2 * head_cols].astype(jnp.bfloat16)
    fresh_values = projected[:, 2 * head_cols:].astype(jnp.bfloat16)
    hidden = jax.nn.gelu(jnp.dot(modulated, w_mlp_in, preferred_element_type=jnp.float32), approximate=True).astype(jnp.bfloat16)
    key_cache = place_rows(key_cache, fresh_keys, first_row, patch_len)
    value_cache = place_rows(value_cache, fresh_values, first_row, patch_len)
    attended = attend(queries, key_cache, value_cache)
    branch = jnp.dot(attended, w_out_attn, preferred_element_type=jnp.float32) + jnp.dot(hidden, w_out_mlp, preferred_element_type=jnp.float32)
    combined = current.astype(jnp.float32) + modulation[2] * branch
    valid_rows = (jnp.arange(current.shape[0], dtype=jnp.int32) < patch_len)[:, None]
    result = jnp.where(valid_rows, combined, 0.0).astype(jnp.float32)
    return (result, key_cache, value_cache)

def reference(activations, modulation, w_qkv, w_mlp_in, w_out_attn, w_out_mlp, key_cache, value_cache, patch_order, patch_lengths):
    section_count = activations.shape[0]
    offsets = (jnp.cumsum(patch_lengths) - patch_lengths).astype(jnp.int32)
    current = activations
    for step_index in range(TICKS):
        patch_id = patch_order[((jnp.arange(section_count, dtype=jnp.int32) - step_index) % section_count).astype(jnp.int32)]
        first_rows = offsets[patch_id].astype(jnp.int32)
        patch_lens = patch_lengths[patch_id].astype(jnp.int32)
        current, key_cache, value_cache = lax.map(section_block, (current, modulation, w_qkv, w_mlp_in, w_out_attn, w_out_mlp, key_cache, value_cache, first_rows, patch_lens))
        if step_index + 1 < TICKS:
            current = jnp.roll(current, 1, axis=0)
    return current
```

```python
import functools
import math

import jax
import jax.numpy as jnp
from jax import lax
from jax.experimental import pallas as pl
from jax.experimental.pallas import tpu as pltpu
from jax.sharding import PartitionSpec as P

HD = 128
TICKS = 2
SIDE = 4
OFFSETS = (0, 1, -1, 2)
NEG = -1e30
SCORE_SCALE = math.log2(math.e) / math.sqrt(HD)
KEY_STEP = 512

norm_eps = 1e-06

VMEM = pl.BlockSpec(memory_space=pltpu.VMEM)
NT = (((1,), (1,)), ((), ()))


def place(section, sp, first_by, second_by):
    x, y = sp // SIDE, sp % SIDE
    if section % 2:
        first_by, second_by = second_by, first_by
    return ((x + first_by) % SIDE) * SIDE + (y + second_by) % SIDE


def received(v, first_by, second_by, sections, width):
    pairs = [
        (s * width + place(s, d, first_by, second_by), s * width + d)
        for s in range(sections)
        for d in range(width)
    ]
    return lax.ppermute(v, ("section", "sp"), pairs)


def sent(v, first_by, second_by, sections, width):
    pairs = [
        (s * width + d, s * width + place(s, d, first_by, second_by))
        for s in range(sections)
        for d in range(width)
    ]
    return lax.ppermute(v, ("section", "sp"), pairs)


def modulate_kernel(current, modulation, out):
    values = current[...].astype(jnp.float32)
    row_mean = jnp.mean(values, axis=-1, keepdims=True)
    centered = values - row_mean
    row_var = jnp.mean(centered * centered, axis=-1, keepdims=True)
    normed = centered * lax.rsqrt(row_var + norm_eps)
    out[...] = (normed * (1.0 + modulation[1:2, :]) + modulation[0:1, :]).astype(out.dtype)


def modulate(current, modulation):
    return pl.pallas_call(
        modulate_kernel,
        out_shape=jax.ShapeDtypeStruct(current.shape, jnp.bfloat16),
        in_specs=[VMEM, VMEM],
        out_specs=VMEM,
        name="modulate",
    )(current, modulation)


def project_kernel(rows, w_qkv, w_inner, q_out, k_out, v_out, hidden_out):
    rows_now = rows[...]

    def times(weight):
        return jnp.dot(rows_now, weight, preferred_element_type=jnp.float32)

    queries = times(w_qkv[0]) * SCORE_SCALE
    high = queries.astype(jnp.bfloat16)
    q_out[:, :HD] = high
    q_out[:, HD:] = (queries - high.astype(jnp.float32)).astype(jnp.bfloat16)
    k_out[...] = times(w_qkv[1]).astype(jnp.bfloat16)
    v_out[...] = times(w_qkv[2]).astype(jnp.bfloat16)
    hidden_out[...] = jax.nn.gelu(times(w_inner[...]), approximate=True).astype(jnp.bfloat16)


def project(rows, w_qkv, w_inner):
    n, d = rows.shape
    units = w_inner.shape[1]
    return pl.pallas_call(
        project_kernel,
        out_shape=[
            jax.ShapeDtypeStruct((n, 2 * HD), jnp.bfloat16),
            jax.ShapeDtypeStruct((n, HD), jnp.bfloat16),
            jax.ShapeDtypeStruct((n, HD), jnp.bfloat16),
            jax.ShapeDtypeStruct((n, units), jnp.bfloat16),
        ],
        in_specs=[VMEM] * 3,
        out_specs=[VMEM] * 4,
        cost_estimate=pl.CostEstimate(
            flops=2 * n * d * (3 * HD + units), bytes_accessed=d * (3 * HD + units) * 2, transcendentals=n * units
        ),
        name="project",
    )(rows, w_qkv, w_inner)


def scores_of(q, keys, bias):
    keys_twice = jnp.concatenate([keys, keys], axis=1)
    return lax.dot_general(q, keys_twice, NT, preferred_element_type=jnp.float32) + bias


def weighted(probs, values):
    ones = jnp.ones(values.shape, jnp.bfloat16)
    return jnp.dot(probs, jnp.concatenate([values, ones], axis=1), preferred_element_type=jnp.float32)


def stale_kernel(q_ref, *refs):
    *sets, top_out, mix_out, held = refs
    q = q_ref[...]
    n = q.shape[0]
    top = jnp.full((n, HD), NEG, jnp.float32)
    spans = []
    at = 0
    for i in range(0, len(sets), 3):
        keys, values, bias = sets[i : i + 3]
        for j in range(0, keys.shape[0], KEY_STEP):
            s = scores_of(q, keys[j : j + KEY_STEP, :], bias[:, j : j + KEY_STEP])
            held[:, at : at + KEY_STEP] = s
            for c in range(0, KEY_STEP, HD):
                top = jnp.maximum(top, s[:, c : c + HD])
            spans.append((at, values, j))
            at += KEY_STEP
    row_top = jnp.max(top, axis=1, keepdims=True)
    mix = jnp.zeros((n, 2 * HD), jnp.float32)
    for at, values, j in spans:
        probs = jnp.exp2(held[:, at : at + KEY_STEP] - row_top).astype(jnp.bfloat16)
        mix = mix + weighted(probs, values[j : j + KEY_STEP, :])
    top_out[...] = jnp.broadcast_to(row_top, top_out.shape)
    mix_out[...] = mix


def stale_attention(q, sets):
    n = q.shape[0]
    total = sum(s[0].shape[0] for s in sets)
    flat = [a for s in sets for a in s]
    return pl.pallas_call(
        stale_kernel,
        out_shape=[
            jax.ShapeDtypeStruct((n, HD), jnp.float32),
            jax.ShapeDtypeStruct((n, 2 * HD), jnp.float32),
        ],
        in_specs=[VMEM] * (1 + len(flat)),
        out_specs=[VMEM] * 2,
        scratch_shapes=[pltpu.VMEM((n, total), jnp.float32)],
        compiler_params=pltpu.CompilerParams(vmem_limit_bytes=24 * 2**20),
        cost_estimate=pl.CostEstimate(
            flops=2 * n * total * 4 * HD, bytes_accessed=total * 2 * HD * 2, transcendentals=n * total
        ),
        name="stale",
    )(q, *flat)


def finish_kernel(q, keys, values, bias, top, mix, hidden, w_attn, w_mlp, gate, out):
    s = scores_of(q[...], keys[...], bias[...])
    old_top = top[:, :1]
    new_top = jnp.maximum(old_top, jnp.max(s, axis=1, keepdims=True))
    probs = jnp.exp2(s - new_top).astype(jnp.bfloat16)
    total = mix[...] * jnp.exp2(old_top - new_top) + weighted(probs, values[...])
    attended = (total[:, :HD] / total[:, HD : HD + 1]).astype(jnp.bfloat16)
    branch = jnp.dot(attended, w_attn[...], preferred_element_type=jnp.float32)
    branch = branch + jnp.dot(hidden[...], w_mlp[...], preferred_element_type=jnp.float32)
    out[...] = (branch * gate[...]).astype(out.dtype)


def finish(q, keys, values, bias, top, mix, hidden, w_attn, w_mlp, gate, dtype):
    n, d = q.shape[0], w_attn.shape[1]
    units = HD + w_mlp.shape[0]
    return pl.pallas_call(
        finish_kernel,
        out_shape=jax.ShapeDtypeStruct((n, d), dtype),
        in_specs=[VMEM] * 10,
        out_specs=VMEM,
        compiler_params=pltpu.CompilerParams(vmem_limit_bytes=24 * 2**20),
        cost_estimate=pl.CostEstimate(
            flops=2 * n * d * units, bytes_accessed=units * d * 2, transcendentals=n * keys.shape[0]
        ),
        name="finish",
    )(q, keys, values, bias, top, mix, hidden, w_attn, w_mlp, gate)


def pick_entry(lookup_table, position):
    slots = jnp.arange(lookup_table.shape[0], dtype=jnp.int32)
    return jnp.sum(jnp.where(slots == position, lookup_table, 0))


def on_device(
    sections,
    width,
    activations,
    modulation,
    w_qkv,
    w_mlp_in,
    w_out_attn,
    w_out_mlp,
    key_cache,
    value_cache,
    patch_order,
    patch_lengths,
):
    section_index = lax.axis_index("section")
    sp_index = lax.axis_index("sp")
    tok_rows = activations.shape[1]
    mod_rows = modulation[0]
    gate = mod_rows[2:3]
    w_joined = jnp.transpose(w_qkv[0], (1, 0, 2))
    w_inner = w_mlp_in[0]
    w_attn = w_out_attn[0]
    w_mlp = w_out_mlp[0]
    keys_all = key_cache[0]
    values_all = value_cache[0]
    seq = keys_all.shape[0]
    offsets = jnp.cumsum(patch_lengths) - patch_lengths

    odd = section_index % 2
    x, y = sp_index // SIDE, sp_index % SIDE
    owners = []
    for second_by in OFFSETS:
        for first_by in OFFSETS:
            x_by = jnp.where(odd == 1, second_by, first_by)
            y_by = jnp.where(odd == 1, first_by, second_by)
            owners.append(((x + x_by) % SIDE) * SIDE + (y + y_by) % SIDE)
    slot_rows = (
        jnp.stack(owners)[:, None] * tok_rows + jnp.arange(tok_rows, dtype=jnp.int32)[None, :]
    ).reshape(1, -1)
    seq_rows = jnp.arange(seq, dtype=jnp.int32)[None, :]

    patches = []
    for step in range(TICKS):
        patch_id = pick_entry(patch_order, (section_index - step) % sections)
        patches.append((patch_id, pick_entry(offsets, patch_id), pick_entry(patch_lengths, patch_id)))

    stale_off = jnp.zeros((1, seq), jnp.bool_)
    older = []
    current = activations[0]
    for step in range(TICKS):
        patch_id, first_row, patch_len = patches[step]
        stale_off = stale_off | ((seq_rows >= first_row) & (seq_rows < first_row + patch_len))
        stale_bias = jnp.where(stale_off, NEG, 0.0).astype(jnp.float32)
        fresh_bias = jnp.where(slot_rows < patch_len, 0.0, NEG).astype(jnp.float32)
        sets = [(keys_all, values_all, stale_bias)]
        for old_id, old_keys, old_values, old_bias in older:
            sets.append((old_keys, old_values, jnp.where(old_id == patch_id, NEG, old_bias)))

        modulated = modulate(current, mod_rows)
        near = [modulated] + [received(modulated, by, 0, sections, width) for by in OFFSETS[1:]]
        near = jnp.concatenate(near, axis=0)
        blocks = [near] + [received(near, 0, by, sections, width) for by in OFFSETS[1:]]
        parts = [project(rows, w_joined, w_inner) for rows in blocks]
        mixes = [stale_attention(p[0], sets) for p in parts]
        fresh_keys = jnp.concatenate([p[1] for p in parts], axis=0)
        fresh_values = jnp.concatenate([p[2] for p in parts], axis=0)

        def branch_of(i, dtype):
            return finish(
                parts[i][0], fresh_keys, fresh_values, fresh_bias, *mixes[i], parts[i][3], w_attn, w_mlp, gate, dtype
            )

        arrived = [
            sent(branch_of(i, jnp.bfloat16), 0, OFFSETS[i], sections, width) for i in range(1, len(OFFSETS))
        ]
        own = branch_of(0, jnp.float32)
        for a in arrived:
            own = own + a.astype(jnp.float32)
        pieces = [own[i * tok_rows : (i + 1) * tok_rows] for i in range(len(OFFSETS))]
        arrived = [
            sent(pieces[i].astype(jnp.bfloat16), OFFSETS[i], 0, sections, width) for i in range(1, len(OFFSETS))
        ]
        result = current.astype(jnp.float32) + pieces[0]
        for a in arrived:
            result = result + a.astype(jnp.float32)
        row_index = sp_index * tok_rows + jnp.arange(tok_rows, dtype=jnp.int32)
        result = jnp.where((row_index < patch_len)[:, None], result, 0.0)
        if step + 1 < TICKS:
            older.append((patch_id, fresh_keys, fresh_values, fresh_bias))
            current = lax.ppermute(
                result.astype(jnp.bfloat16), "section", [(i, (i + 1) % sections) for i in range(sections)]
            )
        else:
            current = result
    return current[None]


def solution(mesh):
    placed = (
        P("section", "sp", None),
        P("section", None, None),
        P("section", None, None, "sp"),
        P("section", None, "sp"),
        P("section", "sp", None),
        P("section", "sp", None),
        P("section", None, "sp"),
        P("section", None, "sp"),
        P(),
        P(),
    )
    return jax.shard_map(
        functools.partial(on_device, mesh.shape["section"], mesh.shape["sp"]),
        mesh=mesh,
        in_specs=placed,
        out_specs=P("section", "sp", None),
        check_vma=False,
    )
```

```python
import functools
import math

import jax
import jax.numpy as jnp
from jax import lax
from jax.experimental import pallas as pl
from jax.experimental.pallas import tpu as pltpu
from jax.sharding import PartitionSpec as P

HD = 128
TICKS = 2
SIDE = 4
OFFSETS = (0, 1, -1, 2)
NEG = -1e30
SCORE_SCALE = math.log2(math.e) / math.sqrt(HD)
KEY_STEP = 512

norm_eps = 1e-06

VMEM = pl.BlockSpec(memory_space=pltpu.VMEM)
SMEM = pl.BlockSpec(memory_space=pltpu.SMEM)
ANY = pl.BlockSpec(memory_space=pl.ANY)
NT = (((1,), (1,)), ((), ()))
BF16 = jnp.bfloat16
NO_COST = pl.CostEstimate(flops=0, bytes_accessed=0, transcendentals=0)
F32 = jnp.float32


def shape(dims, dtype):
    return jax.ShapeDtypeStruct(dims, dtype)


def params(mib):
    return pltpu.CompilerParams(vmem_limit_bytes=mib * 2**20)


def after(value, *others):
    return lax.optimization_barrier((value, others))[0]


def place(section, sp, first_by, second_by):
    x, y = sp // SIDE, sp % SIDE
    if section % 2:
        first_by, second_by = second_by, first_by
    return ((x + first_by) % SIDE) * SIDE + (y + second_by) % SIDE


def received(v, first_by, second_by, sections, width):
    pairs = [
        (s * width + place(s, d, first_by, second_by), s * width + d)
        for s in range(sections)
        for d in range(width)
    ]
    return lax.ppermute(v, ("section", "sp"), pairs)


def sent(v, first_by, second_by, sections, width, section_by=0):
    pairs = [
        (s * width + d, (s + section_by) % sections * width + place(s, d, first_by, second_by))
        for s in range(sections)
        for d in range(width)
    ]
    return lax.ppermute(v, ("section", "sp"), pairs)


def masks_kernel(sections, order, lengths, spot, stale0, stale1, fresh0, fresh1, old1, keep):
    section, sp = spot[0], spot[1]
    tok_rows = keep.shape[0]
    ids, firsts, lens = [], [], []
    for t in range(TICKS):
        patch_id = order[lax.rem(section - t + sections, sections)]
        first = jnp.int32(0)
        for i in range(sections):
            first = first + jnp.where(i < patch_id, lengths[i], 0)
        ids.append(patch_id)
        firsts.append(first)
        lens.append(lengths[patch_id])

    def off(mask):
        return jnp.where(mask, NEG, 0.0).astype(F32)

    rows = lax.broadcasted_iota(jnp.int32, stale0.shape, 1)
    within = [(rows >= f) & (rows < f + n) for f, n in zip(firsts, lens)]
    stale0[...] = off(within[0])
    stale1[...] = off(within[0] | within[1])

    slot = lax.broadcasted_iota(jnp.int32, fresh0.shape, 1)
    block = lax.shift_right_logical(slot, tok_rows.bit_length() - 1)

    def offset(i):
        return jnp.where(i < 2, i, 5 - i)

    first_by = offset(block & (SIDE - 1))
    second_by = offset(lax.shift_right_logical(block, 2))
    odd = (section & 1) == 1
    x = (lax.shift_right_logical(sp, 2) + jnp.where(odd, second_by, first_by)) & (SIDE - 1)
    y = ((sp & (SIDE - 1)) + jnp.where(odd, first_by, second_by)) & (SIDE - 1)
    slot_row = (x * SIDE + y) * tok_rows + (slot & (tok_rows - 1))
    fresh0[...] = off(slot_row >= lens[0])
    fresh1[...] = off(slot_row >= lens[1])
    same = jnp.where(ids[0] == ids[1], 1, 0)
    old1[...] = off((slot_row >= lens[0]) | (slot_row * 0 + same == 1))
    own_row = lax.broadcasted_iota(jnp.int32, keep.shape, 0) + sp * tok_rows
    keep[...] = jnp.where(own_row < lens[1], 1.0, 0.0).astype(F32)


def make_masks(order, lengths, spot, seq, slots, tok_rows, sections):
    return pl.pallas_call(
        functools.partial(masks_kernel, sections),
        out_shape=[shape((1, seq), F32)] * 2 + [shape((1, slots), F32)] * 3 + [shape((tok_rows, HD), F32)],
        in_specs=[SMEM] * 3,
        out_specs=[VMEM] * 6,
        compiler_params=params(4),
        cost_estimate=NO_COST,
        name="masks",
    )(order, lengths, spot)


def side_by_side_kernel(w_qkv, w_inner, out, sems):
    copies = [
        pltpu.make_async_copy(w_qkv.at[i], out.at[:, i * HD : (i + 1) * HD], sems.at[i]) for i in range(3)
    ] + [pltpu.make_async_copy(w_inner, out.at[:, 3 * HD :], sems.at[3])]
    for c in copies:
        c.start()
    for c in copies:
        c.wait()


def side_by_side(w_qkv, w_inner):
    d, units = w_inner.shape
    return pl.pallas_call(
        side_by_side_kernel,
        out_shape=shape((d, 3 * HD + units), BF16),
        in_specs=[ANY] * 2,
        out_specs=VMEM,
        scratch_shapes=[pltpu.SemaphoreType.DMA((4,))],
        compiler_params=params(4),
        cost_estimate=NO_COST,
        name="side_by_side",
    )(w_qkv, w_inner)


def modulated_rows(values, modulation):
    row_mean = jnp.mean(values, axis=-1, keepdims=True)
    centered = values - row_mean
    row_var = jnp.mean(centered * centered, axis=-1, keepdims=True)
    normed = centered * lax.rsqrt(row_var + norm_eps)
    return (normed * (1.0 + modulation[1:2, :]) + modulation[0:1, :]).astype(BF16)


def join_modulated_kernel(modulation, *refs):
    *rows, out = refs
    n = rows[0].shape[0]
    for i, r in enumerate(rows):
        out[i * n : (i + 1) * n, :] = modulated_rows(r[...].astype(F32), modulation)


def join_modulated(modulation, rows):
    n, d = rows[0].shape
    return pl.pallas_call(
        join_modulated_kernel,
        out_shape=shape((n * len(rows), d), BF16),
        in_specs=[VMEM] * (1 + len(rows)),
        out_specs=VMEM,
        compiler_params=params(8),
        cost_estimate=NO_COST,
        name="join_modulated",
    )(modulation, *rows)


def join_kernel(*refs):
    *rows, out = refs
    n = rows[0].shape[0]
    for i, r in enumerate(rows):
        out[i * n : (i + 1) * n, :] = r[...]


def join(rows):
    n, d = rows[0].shape
    return pl.pallas_call(
        join_kernel,
        out_shape=shape((n * len(rows), d), rows[0].dtype),
        in_specs=[VMEM] * len(rows),
        out_specs=VMEM,
        compiler_params=params(4),
        cost_estimate=NO_COST,
        name="join",
    )(*rows)


def summed_modulated_kernel(modulation, *refs):
    *parts, total_out, out = refs
    total = parts[0][...].astype(F32)
    for p in parts[1:]:
        total = total + p[...].astype(F32)
    total_out[...] = total
    out[...] = modulated_rows(total, modulation)


def summed_modulated(modulation, parts):
    n, d = parts[0].shape
    return pl.pallas_call(
        summed_modulated_kernel,
        out_shape=[shape((n, d), F32), shape((n, d), BF16)],
        in_specs=[VMEM] * (1 + len(parts)),
        out_specs=[VMEM] * 2,
        compiler_params=params(4),
        cost_estimate=NO_COST,
        name="summed_modulated",
    )(modulation, *parts)


def project_kernel(weights, *refs):
    *rows, q_out, k_out, v_out, hidden_out = refs
    rows_now = jnp.concatenate([r[...] for r in rows], axis=0) if len(rows) > 1 else rows[0][...]
    product = jnp.dot(rows_now, weights[...], preferred_element_type=F32)
    queries = product[:, :HD] * SCORE_SCALE
    high = queries.astype(BF16)
    q_out[:, :HD] = high
    q_out[:, HD:] = (queries - high.astype(F32)).astype(BF16)
    k_out[...] = product[:, HD : 2 * HD].astype(BF16)
    v_out[...] = product[:, 2 * HD : 3 * HD].astype(BF16)
    hidden_out[...] = jax.nn.gelu(product[:, 3 * HD :], approximate=True).astype(BF16)


def project(weights, rows):
    n = sum(r.shape[0] for r in rows)
    d, columns = weights.shape
    units = columns - 3 * HD
    return pl.pallas_call(
        project_kernel,
        out_shape=[shape((n, c), BF16) for c in (2 * HD, HD, HD, units)],
        in_specs=[VMEM] * (1 + len(rows)),
        out_specs=[VMEM] * 4,
        compiler_params=params(8),
        cost_estimate=NO_COST,
        name="project",
    )(weights, *rows)


def scores_of(q, keys, bias):
    keys_twice = jnp.concatenate([keys, keys], axis=1)
    return lax.dot_general(q, keys_twice, NT, preferred_element_type=F32) + bias


def weighted(probs, values):
    return jnp.dot(probs, jnp.concatenate([values, jnp.ones_like(values)], axis=1), preferred_element_type=F32)


def stale_kernel(step, q_ref, *refs):
    *sets, top_out, mix_out = refs
    q = q_ref[...]
    n = q.shape[0]
    top = jnp.full((n, 1), NEG, F32)
    mix = jnp.zeros((n, 2 * HD), F32)
    for i in range(0, len(sets), 3):
        keys, values, bias = sets[i : i + 3]
        total = keys.shape[0]
        for j in range(0, total, min(step, total)):
            span = slice(j, j + min(step, total))
            s = scores_of(q, keys[span, :], bias[:, span])
            new_top = jnp.maximum(top, jnp.max(s, axis=1, keepdims=True))
            probs = jnp.exp2(s - new_top).astype(BF16)
            mix = mix * jnp.exp2(top - new_top) + weighted(probs, values[span, :])
            top = new_top
    top_out[...] = jnp.broadcast_to(top, top_out.shape)
    mix_out[...] = mix


def stale_attention(q, sets):
    n = q.shape[0]
    total = sum(s[0].shape[0] for s in sets)
    flat = [a for s in sets for a in s]
    return pl.pallas_call(
        functools.partial(stale_kernel, 512 if n >= 256 else 2048),
        out_shape=[shape((n, HD), F32), shape((n, 2 * HD), F32)],
        in_specs=[VMEM] * (1 + len(flat)),
        out_specs=[VMEM] * 2,
        compiler_params=params(12),
        cost_estimate=NO_COST,
        name="stale",
    )(q, *flat)


def finish_kernel(at, sizes, q, top, mix, hidden, modulation, w_attn, w_mlp, bias, *refs):
    outs = refs[-len(sizes) :]
    count = (len(refs) - len(sizes)) // 2
    keys = jnp.concatenate([r[...] for r in refs[:count]], axis=0)
    values = jnp.concatenate([r[...] for r in refs[count : 2 * count]], axis=0)
    span = slice(at, at + sum(sizes))
    s = scores_of(q[span, :], keys, bias[...])
    old_top = top[span, :1]
    new_top = jnp.maximum(old_top, jnp.max(s, axis=1, keepdims=True))
    probs = jnp.exp2(s - new_top).astype(BF16)
    total = mix[span, :] * jnp.exp2(old_top - new_top) + weighted(probs, values)
    attended = (total[:, :HD] / total[:, HD : HD + 1]).astype(BF16)
    branch = jnp.dot(attended, w_attn[...], preferred_element_type=F32)
    branch = branch + jnp.dot(hidden[span, :], w_mlp[...], preferred_element_type=F32)
    branch = branch * modulation[2:3, :]
    begin = 0
    for n, out in zip(sizes, outs):
        out[...] = branch[begin : begin + n, :].astype(out.dtype)
        begin += n


def finish(at, sizes, dtypes, part, mixed, modulation, w_attn, w_mlp, bias, keys, values):
    d = w_attn.shape[1]
    return pl.pallas_call(
        functools.partial(finish_kernel, at, sizes),
        out_shape=[shape((n, d), t) for n, t in zip(sizes, dtypes)],
        in_specs=[VMEM] * (8 + 2 * len(keys)),
        out_specs=[VMEM] * len(sizes),
        compiler_params=params(8),
        cost_estimate=NO_COST,
        name="finish",
    )(part[0], *mixed, part[3], modulation, w_attn, w_mlp, bias, *keys, *values)


def add_kernel(total, arrived, out):
    out[...] = total[...] + arrived[...].astype(F32)


def add(total, arrived):
    return pl.pallas_call(
        add_kernel,
        out_shape=shape(total.shape, F32),
        in_specs=[VMEM] * 2,
        out_specs=VMEM,
        compiler_params=params(4),
        cost_estimate=pl.CostEstimate(flops=2 * 10**9, bytes_accessed=0, transcendentals=0),
        name="add",
    )(total, arrived)


def split_sum_kernel(current, own, *refs):
    count = own.shape[0] // current.shape[0]
    arrived, outs = refs[:-count], refs[-count:]
    n = current.shape[0]
    for i, out in enumerate(outs):
        span = slice(i * n, (i + 1) * n)
        total = own[span, :]
        for a in arrived:
            total = total + a[span, :].astype(F32)
        if i == 0:
            total = total + current[...].astype(F32)
        out[...] = total.astype(out.dtype)


def split_sum(current, own, arrived, first_dtype):
    n, d = current.shape
    dtypes = [first_dtype] + [BF16] * (own.shape[0] // n - 1)
    return pl.pallas_call(
        split_sum_kernel,
        out_shape=[shape((n, d), t) for t in dtypes],
        in_specs=[VMEM] * (2 + len(arrived)),
        out_specs=[VMEM] * len(dtypes),
        compiler_params=params(4),
        cost_estimate=NO_COST,
        name="split_sum",
    )(current, own, *arrived)


def last_sum_kernel(keep, *refs):
    *arrived, out = refs
    total = arrived[0][...].astype(F32)
    for a in arrived[1:]:
        total = total + a[...].astype(F32)
    out[...] = jnp.where(keep[:, :1] > 0.0, total, 0.0)


def last_sum(keep, parts):
    return pl.pallas_call(
        last_sum_kernel,
        out_shape=shape(parts[0].shape, F32),
        in_specs=[VMEM] * (1 + len(parts)),
        out_specs=VMEM,
        compiler_params=params(4),
        cost_estimate=NO_COST,
        name="last_sum",
    )(keep, *parts)


def on_device(
    sections,
    width,
    activations,
    modulation,
    w_qkv,
    w_mlp_in,
    w_out_attn,
    w_out_mlp,
    key_cache,
    value_cache,
    patch_order,
    patch_lengths,
):
    tok_rows = activations.shape[1]
    mod_rows = modulation[0]
    w_attn = w_out_attn[0]
    w_mlp = w_out_mlp[0]
    keys_all = key_cache[0]
    values_all = value_cache[0]
    others = OFFSETS[1:]

    raw = activations[0]
    near = join_modulated(mod_rows, [raw] + [received(raw, by, 0, sections, width) for by in others])

    spot = jnp.stack([lax.axis_index("section"), lax.axis_index("sp")]).astype(jnp.int32)
    stale0, stale1, fresh0, fresh1, old1, keep = make_masks(
        patch_order, patch_lengths, after(spot, near), keys_all.shape[0], tok_rows * width, tok_rows, sections
    )
    weights = side_by_side(jnp.transpose(w_qkv[0], (1, 0, 2)), after(w_mlp_in[0], near))
    stale_bias = (stale0, stale1)
    fresh_bias = (fresh0, fresh1)

    old_sets = []
    current = raw
    n = near.shape[0]
    for step in range(TICKS):
        sets = [(keys_all, values_all, stale_bias[step])] + old_sets
        far1 = received(near, 0, others[0], sections, width)
        far2 = received(near, 0, others[1], sections, width)
        part0 = project(weights, [near])
        mixed0 = stale_attention(part0[0], sets)
        far3 = received(after(near, mixed0), 0, others[2], sections, width)
        part1 = project(weights, after([far1, far2], mixed0))
        mixed1 = stale_attention(part1[0], sets)
        part2 = project(weights, [after(far3, mixed1)])
        keys = [part0[1], part1[1], part2[1]]
        values = [part0[2], part1[2], part2[2]]

        def branch_of(at, dtype, part, mixed):
            return finish(
                at, [n], [dtype], part, mixed, mod_rows, w_attn, w_mlp, fresh_bias[step], keys, values
            )[0]

        out1 = branch_of(0, BF16, part1, mixed1)
        back1 = sent(out1, 0, others[0], sections, width)
        out2 = branch_of(n, BF16, after(part1, out1), mixed1)
        back2 = sent(out2, 0, others[1], sections, width)
        mixed2 = stale_attention(after(part2[0], out2), sets)
        out3 = branch_of(0, BF16, part2, mixed2)
        back3 = sent(out3, 0, others[2], sections, width)
        own = branch_of(0, F32, after(part0, out3), mixed0)
        total = add(add(own, back1), back2)
        last = step + 1 == TICKS
        pieces = split_sum(current, total, [back3], F32 if last else BF16)
        if last:
            arrived = [sent(p, by, 0, sections, width) for p, by in zip(pieces[1:], others)]
            return last_sum(keep, [pieces[0], *arrived])[None]
        arrived = [sent(p, by, 0, sections, width, 1) for p, by in zip(pieces[1:], others)]
        arrived.append(lax.ppermute(pieces[0], "section", [(i, (i + 1) % sections) for i in range(sections)]))
        current, modulated = summed_modulated(mod_rows, arrived)
        old_sets = list(zip(keys, values, jnp.split(old1, [n, 3 * n], axis=1)))
        near = join([modulated] + [received(modulated, by, 0, sections, width) for by in others])


def solution(mesh):
    placed = (
        P("section", "sp", None),
        P("section", None, None),
        P("section", None, None, "sp"),
        P("section", None, "sp"),
        P("section", "sp", None),
        P("section", "sp", None),
        P("section", None, "sp"),
        P("section", None, "sp"),
        P(),
        P(),
    )
    return jax.shard_map(
        functools.partial(on_device, mesh.shape["section"], mesh.shape["sp"]),
        mesh=mesh,
        in_specs=placed,
        out_specs=P("section", "sp", None),
        check_vma=False,
    )
```

```python
import functools
import math

import jax
import jax.numpy as jnp
from jax import lax
from jax.experimental import pallas as pl
from jax.experimental.pallas import tpu as pltpu
from jax.sharding import PartitionSpec as P

HD = 128
TICKS = 2
SIDE = 4
OFFSETS = (0, 1, -1, 2)
NEG = -1e30
SCORE_SCALE = math.log2(math.e) / math.sqrt(HD)
KEY_STEP = 512

norm_eps = 1e-06

VMEM = pl.BlockSpec(memory_space=pltpu.VMEM)
SMEM = pl.BlockSpec(memory_space=pltpu.SMEM)
ANY = pl.BlockSpec(memory_space=pl.ANY)
NT = (((1,), (1,)), ((), ()))
BF16 = jnp.bfloat16
NO_COST = pl.CostEstimate(flops=0, bytes_accessed=0, transcendentals=0)
F32 = jnp.float32


def shape(dims, dtype):
    return jax.ShapeDtypeStruct(dims, dtype)


def params(mib):
    return pltpu.CompilerParams(vmem_limit_bytes=mib * 2**20)


def after(value, *others):
    return lax.optimization_barrier((value, others))[0]


def place(section, sp, first_by, second_by):
    x, y = sp // SIDE, sp % SIDE
    if section % 2:
        first_by, second_by = second_by, first_by
    return ((x + first_by) % SIDE) * SIDE + (y + second_by) % SIDE


def received(v, first_by, second_by, sections, width):
    pairs = [
        (s * width + place(s, d, first_by, second_by), s * width + d)
        for s in range(sections)
        for d in range(width)
    ]
    return lax.ppermute(v, ("section", "sp"), pairs)


def sent(v, first_by, second_by, sections, width, section_by=0):
    pairs = [
        (s * width + d, (s + section_by) % sections * width + place(s, d, first_by, second_by))
        for s in range(sections)
        for d in range(width)
    ]
    return lax.ppermute(v, ("section", "sp"), pairs)


def masks_kernel(sections, order, lengths, spot, stale0, stale1, fresh0, fresh1, old1, keep):
    section, sp = spot[0], spot[1]
    tok_rows = keep.shape[0]
    ids, firsts, lens = [], [], []
    for t in range(TICKS):
        patch_id = order[lax.rem(section - t + sections, sections)]
        first = jnp.int32(0)
        for i in range(sections):
            first = first + jnp.where(i < patch_id, lengths[i], 0)
        ids.append(patch_id)
        firsts.append(first)
        lens.append(lengths[patch_id])

    def off(mask):
        return jnp.where(mask, NEG, 0.0).astype(F32)

    rows = lax.broadcasted_iota(jnp.int32, stale0.shape, 1)
    within = [(rows >= f) & (rows < f + n) for f, n in zip(firsts, lens)]
    stale0[...] = off(within[0])
    stale1[...] = off(within[0] | within[1])

    slot = lax.broadcasted_iota(jnp.int32, fresh0.shape, 1)
    block = lax.shift_right_logical(slot, tok_rows.bit_length() - 1)

    def offset(i):
        return jnp.where(i < 2, i, 5 - i)

    first_by = offset(block & (SIDE - 1))
    second_by = offset(lax.shift_right_logical(block, 2))
    odd = (section & 1) == 1
    x = (lax.shift_right_logical(sp, 2) + jnp.where(odd, second_by, first_by)) & (SIDE - 1)
    y = ((sp & (SIDE - 1)) + jnp.where(odd, first_by, second_by)) & (SIDE - 1)
    slot_row = (x * SIDE + y) * tok_rows + (slot & (tok_rows - 1))
    fresh0[...] = off(slot_row >= lens[0])
    fresh1[...] = off(slot_row >= lens[1])
    same = jnp.where(ids[0] == ids[1], 1, 0)
    old1[...] = off((slot_row >= lens[0]) | (slot_row * 0 + same == 1))
    own_row = lax.broadcasted_iota(jnp.int32, keep.shape, 0) + sp * tok_rows
    keep[...] = jnp.where(own_row < lens[1], 1.0, 0.0).astype(F32)


def make_masks(order, lengths, spot, seq, slots, tok_rows, sections):
    return pl.pallas_call(
        functools.partial(masks_kernel, sections),
        out_shape=[shape((1, seq), F32)] * 2 + [shape((1, slots), F32)] * 3 + [shape((tok_rows, HD), F32)],
        in_specs=[SMEM] * 3,
        out_specs=[VMEM] * 6,
        compiler_params=params(4),
        cost_estimate=NO_COST,
        name="masks",
    )(order, lengths, spot)


def side_by_side_kernel(w_qkv, w_inner, out, sems):
    copies = [
        pltpu.make_async_copy(w_qkv.at[i], out.at[:, i * HD : (i + 1) * HD], sems.at[i]) for i in range(3)
    ] + [pltpu.make_async_copy(w_inner, out.at[:, 3 * HD :], sems.at[3])]
    for c in copies:
        c.start()
    for c in copies:
        c.wait()


def side_by_side(w_qkv, w_inner):
    d, units = w_inner.shape
    return pl.pallas_call(
        side_by_side_kernel,
        out_shape=shape((d, 3 * HD + units), BF16),
        in_specs=[ANY] * 2,
        out_specs=VMEM,
        scratch_shapes=[pltpu.SemaphoreType.DMA((4,))],
        compiler_params=params(4),
        cost_estimate=NO_COST,
        name="side_by_side",
    )(w_qkv, w_inner)


def modulated_rows(values, modulation):
    row_mean = jnp.mean(values, axis=-1, keepdims=True)
    centered = values - row_mean
    row_var = jnp.mean(centered * centered, axis=-1, keepdims=True)
    normed = centered * lax.rsqrt(row_var + norm_eps)
    return (normed * (1.0 + modulation[1:2, :]) + modulation[0:1, :]).astype(BF16)


def join_modulated_kernel(modulation, *refs):
    *rows, low, high = refs
    n = rows[0].shape[0]
    for i, r in enumerate(rows):
        out, at = (low, i) if i < len(rows) // 2 else (high, i - len(rows) // 2)
        out[at * n : (at + 1) * n, :] = modulated_rows(r[...].astype(F32), modulation)


def join_modulated(modulation, rows):
    n, d = rows[0].shape
    return pl.pallas_call(
        join_modulated_kernel,
        out_shape=[shape((n * len(rows) // 2, d), BF16)] * 2,
        in_specs=[VMEM] * (1 + len(rows)),
        out_specs=[VMEM] * 2,
        compiler_params=params(8),
        cost_estimate=NO_COST,
        name="join_modulated",
    )(modulation, *rows)


def join_kernel(*refs):
    *rows, low, high = refs
    n = rows[0].shape[0]
    for i, r in enumerate(rows):
        out, at = (low, i) if i < len(rows) // 2 else (high, i - len(rows) // 2)
        out[at * n : (at + 1) * n, :] = r[...]


def join(rows):
    n, d = rows[0].shape
    return pl.pallas_call(
        join_kernel,
        out_shape=[shape((n * len(rows) // 2, d), rows[0].dtype)] * 2,
        in_specs=[VMEM] * len(rows),
        out_specs=[VMEM] * 2,
        compiler_params=params(4),
        cost_estimate=NO_COST,
        name="join",
    )(*rows)


def summed_modulated_kernel(modulation, *refs):
    *parts, total_out, out = refs
    total = parts[0][...].astype(F32)
    for p in parts[1:]:
        total = total + p[...].astype(F32)
    total_out[...] = total
    out[...] = modulated_rows(total, modulation)


def summed_modulated(modulation, parts):
    n, d = parts[0].shape
    return pl.pallas_call(
        summed_modulated_kernel,
        out_shape=[shape((n, d), F32), shape((n, d), BF16)],
        in_specs=[VMEM] * (1 + len(parts)),
        out_specs=[VMEM] * 2,
        compiler_params=params(4),
        cost_estimate=NO_COST,
        name="summed_modulated",
    )(modulation, *parts)


def project_kernel(weights, *refs):
    *rows, q_out, k_out, v_out, hidden_out = refs
    rows_now = jnp.concatenate([r[...] for r in rows], axis=0) if len(rows) > 1 else rows[0][...]
    product = jnp.dot(rows_now, weights[...], preferred_element_type=F32)
    queries = product[:, :HD] * SCORE_SCALE
    high = queries.astype(BF16)
    q_out[:, :HD] = high
    q_out[:, HD:] = (queries - high.astype(F32)).astype(BF16)
    k_out[...] = product[:, HD : 2 * HD].astype(BF16)
    v_out[...] = product[:, 2 * HD : 3 * HD].astype(BF16)
    hidden_out[...] = jax.nn.gelu(product[:, 3 * HD :], approximate=True).astype(BF16)


def project(weights, rows):
    n = sum(r.shape[0] for r in rows)
    d, columns = weights.shape
    units = columns - 3 * HD
    return pl.pallas_call(
        project_kernel,
        out_shape=[shape((n, c), BF16) for c in (2 * HD, HD, HD, units)],
        in_specs=[VMEM] * (1 + len(rows)),
        out_specs=[VMEM] * 4,
        compiler_params=params(8),
        cost_estimate=NO_COST,
        name="project",
    )(weights, *rows)


def scores_of(q, keys, bias):
    keys_twice = jnp.concatenate([keys, keys], axis=1)
    return lax.dot_general(q, keys_twice, NT, preferred_element_type=F32) + bias


def weighted(probs, values):
    return jnp.dot(probs, jnp.concatenate([values, jnp.ones_like(values)], axis=1), preferred_element_type=F32)


def stale_kernel(step, q_ref, *refs):
    *sets, top_out, mix_out = refs
    q = q_ref[...]
    n = q.shape[0]
    top = jnp.full((n, 1), NEG, F32)
    mix = jnp.zeros((n, 2 * HD), F32)
    for i in range(0, len(sets), 3):
        keys, values, bias = sets[i : i + 3]
        total = keys.shape[0]
        for j in range(0, total, min(step, total)):
            span = slice(j, j + min(step, total))
            s = scores_of(q, keys[span, :], bias[:, span])
            new_top = jnp.maximum(top, jnp.max(s, axis=1, keepdims=True))
            probs = jnp.exp2(s - new_top).astype(BF16)
            mix = mix * jnp.exp2(top - new_top) + weighted(probs, values[span, :])
            top = new_top
    top_out[...] = jnp.broadcast_to(top, top_out.shape)
    mix_out[...] = mix


def stale_attention(q, sets):
    n = q.shape[0]
    total = sum(s[0].shape[0] for s in sets)
    flat = [a for s in sets for a in s]
    return pl.pallas_call(
        functools.partial(stale_kernel, 512 if n >= 256 else 2048),
        out_shape=[shape((n, HD), F32), shape((n, 2 * HD), F32)],
        in_specs=[VMEM] * (1 + len(flat)),
        out_specs=[VMEM] * 2,
        compiler_params=params(12),
        cost_estimate=NO_COST,
        name="stale",
    )(q, *flat)


def finish_kernel(at, sizes, q, top, mix, hidden, modulation, w_attn, w_mlp, bias, *refs):
    outs = refs[-len(sizes) :]
    count = (len(refs) - len(sizes)) // 2
    keys = jnp.concatenate([r[...] for r in refs[:count]], axis=0)
    values = jnp.concatenate([r[...] for r in refs[count : 2 * count]], axis=0)
    span = slice(at, at + sum(sizes))
    s = scores_of(q[span, :], keys, bias[...])
    old_top = top[span, :1]
    new_top = jnp.maximum(old_top, jnp.max(s, axis=1, keepdims=True))
    probs = jnp.exp2(s - new_top).astype(BF16)
    total = mix[span, :] * jnp.exp2(old_top - new_top) + weighted(probs, values)
    attended = (total[:, :HD] / total[:, HD : HD + 1]).astype(BF16)
    branch = jnp.dot(attended, w_attn[...], preferred_element_type=F32)
    branch = branch + jnp.dot(hidden[span, :], w_mlp[...], preferred_element_type=F32)
    branch = branch * modulation[2:3, :]
    begin = 0
    for n, out in zip(sizes, outs):
        out[...] = branch[begin : begin + n, :].astype(out.dtype)
        begin += n


def finish(at, sizes, dtypes, part, mixed, modulation, w_attn, w_mlp, bias, keys, values):
    d = w_attn.shape[1]
    return pl.pallas_call(
        functools.partial(finish_kernel, at, sizes),
        out_shape=[shape((n, d), t) for n, t in zip(sizes, dtypes)],
        in_specs=[VMEM] * (8 + 2 * len(keys)),
        out_specs=[VMEM] * len(sizes),
        compiler_params=params(8),
        cost_estimate=NO_COST,
        name="finish",
    )(part[0], *mixed, part[3], modulation, w_attn, w_mlp, bias, *keys, *values)


def add_kernel(total, arrived, out):
    out[...] = total[...] + arrived[...].astype(F32)


def add(total, arrived):
    return pl.pallas_call(
        add_kernel,
        out_shape=shape(total.shape, F32),
        in_specs=[VMEM] * 2,
        out_specs=VMEM,
        compiler_params=params(4),
        cost_estimate=pl.CostEstimate(flops=2 * 10**9, bytes_accessed=0, transcendentals=0),
        name="add",
    )(total, arrived)


def split_sum_kernel(current, own, *refs):
    count = own.shape[0] // current.shape[0]
    arrived, outs = refs[:-count], refs[-count:]
    n = current.shape[0]
    for i, out in enumerate(outs):
        span = slice(i * n, (i + 1) * n)
        total = own[span, :]
        for a in arrived:
            total = total + a[span, :].astype(F32)
        if i == 0:
            total = total + current[...].astype(F32)
        out[...] = total.astype(out.dtype)


def split_sum(current, own, arrived, first_dtype):
    n, d = current.shape
    dtypes = [first_dtype] + [BF16] * (own.shape[0] // n - 1)
    return pl.pallas_call(
        split_sum_kernel,
        out_shape=[shape((n, d), t) for t in dtypes],
        in_specs=[VMEM] * (2 + len(arrived)),
        out_specs=[VMEM] * len(dtypes),
        compiler_params=params(4),
        cost_estimate=NO_COST,
        name="split_sum",
    )(current, own, *arrived)


def last_sum_kernel(keep, *refs):
    *arrived, out = refs
    total = arrived[0][...].astype(F32)
    for a in arrived[1:]:
        total = total + a[...].astype(F32)
    out[...] = jnp.where(keep[:, :1] > 0.0, total, 0.0)


def last_sum(keep, parts):
    return pl.pallas_call(
        last_sum_kernel,
        out_shape=shape(parts[0].shape, F32),
        in_specs=[VMEM] * (1 + len(parts)),
        out_specs=VMEM,
        compiler_params=params(4),
        cost_estimate=NO_COST,
        name="last_sum",
    )(keep, *parts)


def on_device(
    sections,
    width,
    activations,
    modulation,
    w_qkv,
    w_mlp_in,
    w_out_attn,
    w_out_mlp,
    key_cache,
    value_cache,
    patch_order,
    patch_lengths,
):
    tok_rows = activations.shape[1]
    mod_rows = modulation[0]
    w_attn = w_out_attn[0]
    w_mlp = w_out_mlp[0]
    keys_all = key_cache[0]
    values_all = value_cache[0]
    others = OFFSETS[1:]

    raw = activations[0]
    raw_near = [raw] + [received(raw, by, 0, sections, width) for by in others]

    spot = jnp.stack([lax.axis_index("section"), lax.axis_index("sp")]).astype(jnp.int32)
    stale0, stale1, fresh0, fresh1, old1, keep = make_masks(
        patch_order, patch_lengths, spot, keys_all.shape[0], tok_rows * width, tok_rows, sections
    )
    weights = side_by_side(jnp.transpose(w_qkv[0], (1, 0, 2)), w_mlp_in[0])
    near = join_modulated(mod_rows, after(raw_near, weights, stale0))
    stale_bias = (stale0, stale1)
    fresh_bias = (fresh0, fresh1)

    old_sets = []
    current = raw
    n = tok_rows * SIDE
    for step in range(TICKS):
        sets = [(keys_all, values_all, stale_bias[step])] + old_sets
        low, high = near
        low_next = received(low, 0, 1, sections, width)
        high_prev = received(high, 0, -1, sections, width)
        high_next = received(high, 0, 1, sections, width)
        low_prev = received(low, 0, -1, sections, width)
        low_far = received(low_next, 0, 1, sections, width)
        high_far = received(high_prev, 0, -1, sections, width)
        part0 = project(weights, [low, high])
        mixed0 = stale_attention(part0[0], sets)
        part1 = project(weights, after([low_next, high_next, low_prev, high_prev], mixed0))
        mixed1 = stale_attention(part1[0], sets)
        part2 = project(weights, after([low_far, high_far], mixed1))
        keys = [part0[1], part1[1], part2[1]]
        values = [part0[2], part1[2], part2[2]]

        def branch_of(at, dtype, part, mixed):
            return finish(
                at, [n], [dtype], part, mixed, mod_rows, w_attn, w_mlp, fresh_bias[step], keys, values
            )[0]

        out1 = branch_of(0, BF16, part1, mixed1)
        back1 = sent(out1, 0, others[0], sections, width)
        out2 = branch_of(n, BF16, after(part1, out1), mixed1)
        back2 = sent(out2, 0, others[1], sections, width)
        mixed2 = stale_attention(after(part2[0], out2), sets)
        out3 = branch_of(0, BF16, part2, mixed2)
        back3 = sent(out3, 0, others[2], sections, width)
        own = branch_of(0, F32, after(part0, out3), mixed0)
        total = add(add(own, back1), back2)
        last = step + 1 == TICKS
        pieces = split_sum(current, total, [back3], F32 if last else BF16)
        if last:
            arrived = [sent(p, by, 0, sections, width) for p, by in zip(pieces[1:], others)]
            return last_sum(keep, [pieces[0], *arrived])[None]
        arrived = [sent(p, by, 0, sections, width, 1) for p, by in zip(pieces[1:], others)]
        arrived.append(lax.ppermute(pieces[0], "section", [(i, (i + 1) % sections) for i in range(sections)]))
        current, modulated = summed_modulated(mod_rows, arrived)
        old_sets = list(zip(keys, values, jnp.split(old1, [n, 3 * n], axis=1)))
        near = join([modulated] + [received(modulated, by, 0, sections, width) for by in others])


def solution(mesh):
    placed = (
        P("section", "sp", None),
        P("section", None, None),
        P("section", None, None, "sp"),
        P("section", None, "sp"),
        P("section", "sp", None),
        P("section", "sp", None),
        P("section", None, "sp"),
        P("section", None, "sp"),
        P(),
        P(),
    )
    return jax.shard_map(
        functools.partial(on_device, mesh.shape["section"], mesh.shape["sp"]),
        mesh=mesh,
        in_specs=placed,
        out_specs=P("section", "sp", None),
        check_vma=False,
    )
```

```python
import functools
import math

import jax
import jax.numpy as jnp
from jax import lax
from jax.experimental import pallas as pl
from jax.experimental.pallas import tpu as pltpu
from jax.sharding import PartitionSpec as P

HD = 128
TICKS = 2
SIDE = 4
OFFSETS = (0, 1, -1, 2)
NEG = -1e30
SCORE_SCALE = math.log2(math.e) / math.sqrt(HD)
KEY_STEP = 512

norm_eps = 1e-06

VMEM = pl.BlockSpec(memory_space=pltpu.VMEM)
SMEM = pl.BlockSpec(memory_space=pltpu.SMEM)
ANY = pl.BlockSpec(memory_space=pl.ANY)
NT = (((1,), (1,)), ((), ()))
BF16 = jnp.bfloat16
NO_COST = pl.CostEstimate(flops=0, bytes_accessed=0, transcendentals=0)
F32 = jnp.float32


def shape(dims, dtype):
    return jax.ShapeDtypeStruct(dims, dtype)


def params(mib):
    return pltpu.CompilerParams(vmem_limit_bytes=mib * 2**20)


def after(value, *others):
    return lax.optimization_barrier((value, others))[0]


def place(section, sp, first_by, second_by):
    x, y = sp // SIDE, sp % SIDE
    if section % 2:
        first_by, second_by = second_by, first_by
    return ((x + first_by) % SIDE) * SIDE + (y + second_by) % SIDE


def received(v, first_by, second_by, sections, width):
    pairs = [
        (s * width + place(s, d, first_by, second_by), s * width + d)
        for s in range(sections)
        for d in range(width)
    ]
    return lax.ppermute(v, ("section", "sp"), pairs)


def sent(v, first_by, second_by, sections, width, section_by=0):
    pairs = [
        (s * width + d, (s + section_by) % sections * width + place(s, d, first_by, second_by))
        for s in range(sections)
        for d in range(width)
    ]
    return lax.ppermute(v, ("section", "sp"), pairs)


def masks_kernel(sections, order, lengths, spot, stale0, stale1, fresh0, fresh1, old1, keep):
    section, sp = spot[0], spot[1]
    tok_rows = keep.shape[0]
    ids, firsts, lens = [], [], []
    for t in range(TICKS):
        patch_id = order[lax.rem(section - t + sections, sections)]
        first = jnp.int32(0)
        for i in range(sections):
            first = first + jnp.where(i < patch_id, lengths[i], 0)
        ids.append(patch_id)
        firsts.append(first)
        lens.append(lengths[patch_id])

    def off(mask):
        return jnp.where(mask, NEG, 0.0).astype(F32)

    rows = lax.broadcasted_iota(jnp.int32, stale0.shape, 1)
    within = [(rows >= f) & (rows < f + n) for f, n in zip(firsts, lens)]
    stale0[...] = off(within[0])
    stale1[...] = off(within[0] | within[1])

    slot = lax.broadcasted_iota(jnp.int32, fresh0.shape, 1)
    block = lax.shift_right_logical(slot, tok_rows.bit_length() - 1)

    def offset(i):
        return jnp.where(i < 2, i, 5 - i)

    first_by = offset(block & (SIDE - 1))
    second_by = offset(lax.shift_right_logical(block, 2))
    odd = (section & 1) == 1
    x = (lax.shift_right_logical(sp, 2) + jnp.where(odd, second_by, first_by)) & (SIDE - 1)
    y = ((sp & (SIDE - 1)) + jnp.where(odd, first_by, second_by)) & (SIDE - 1)
    slot_row = (x * SIDE + y) * tok_rows + (slot & (tok_rows - 1))
    fresh0[...] = off(slot_row >= lens[0])
    fresh1[...] = off(slot_row >= lens[1])
    same = jnp.where(ids[0] == ids[1], 1, 0)
    old1[...] = off((slot_row >= lens[0]) | (slot_row * 0 + same == 1))
    own_row = lax.broadcasted_iota(jnp.int32, keep.shape, 0) + sp * tok_rows
    keep[...] = jnp.where(own_row < lens[1], 1.0, 0.0).astype(F32)


def make_masks(order, lengths, spot, seq, slots, tok_rows, sections):
    return pl.pallas_call(
        functools.partial(masks_kernel, sections),
        out_shape=[shape((1, seq), F32)] * 2 + [shape((1, slots), F32)] * 3 + [shape((tok_rows, HD), F32)],
        in_specs=[SMEM] * 3,
        out_specs=[VMEM] * 6,
        compiler_params=params(4),
        cost_estimate=NO_COST,
        name="masks",
    )(order, lengths, spot)


def side_by_side_kernel(w_qkv, w_inner, out, sems):
    copies = [
        pltpu.make_async_copy(w_qkv.at[i], out.at[:, i * HD : (i + 1) * HD], sems.at[i]) for i in range(3)
    ] + [pltpu.make_async_copy(w_inner, out.at[:, 3 * HD :], sems.at[3])]
    for c in copies:
        c.start()
    for c in copies:
        c.wait()


def side_by_side(w_qkv, w_inner):
    d, units = w_inner.shape
    return pl.pallas_call(
        side_by_side_kernel,
        out_shape=shape((d, 3 * HD + units), BF16),
        in_specs=[ANY] * 2,
        out_specs=VMEM,
        scratch_shapes=[pltpu.SemaphoreType.DMA((4,))],
        compiler_params=params(4),
        cost_estimate=NO_COST,
        name="side_by_side",
    )(w_qkv, w_inner)


def modulated_rows(values, modulation):
    row_mean = jnp.mean(values, axis=-1, keepdims=True)
    centered = values - row_mean
    row_var = jnp.mean(centered * centered, axis=-1, keepdims=True)
    normed = centered * lax.rsqrt(row_var + norm_eps)
    return (normed * (1.0 + modulation[1:2, :]) + modulation[0:1, :]).astype(BF16)


def join_modulated_kernel(modulation, *refs):
    *rows, low, high = refs
    n = rows[0].shape[0]
    for i, r in enumerate(rows):
        out, at = (low, i) if i < len(rows) // 2 else (high, i - len(rows) // 2)
        out[at * n : (at + 1) * n, :] = modulated_rows(r[...].astype(F32), modulation)


def join_modulated(modulation, rows):
    n, d = rows[0].shape
    return pl.pallas_call(
        join_modulated_kernel,
        out_shape=[shape((n * len(rows) // 2, d), BF16)] * 2,
        in_specs=[VMEM] * (1 + len(rows)),
        out_specs=[VMEM] * 2,
        compiler_params=params(8),
        cost_estimate=NO_COST,
        name="join_modulated",
    )(modulation, *rows)


def join_kernel(*refs):
    *rows, low, high = refs
    n = rows[0].shape[0]
    for i, r in enumerate(rows):
        out, at = (low, i) if i < len(rows) // 2 else (high, i - len(rows) // 2)
        out[at * n : (at + 1) * n, :] = r[...]


def join(rows):
    n, d = rows[0].shape
    return pl.pallas_call(
        join_kernel,
        out_shape=[shape((n * len(rows) // 2, d), rows[0].dtype)] * 2,
        in_specs=[VMEM] * len(rows),
        out_specs=[VMEM] * 2,
        compiler_params=params(4),
        cost_estimate=NO_COST,
        name="join",
    )(*rows)


def summed_modulated_kernel(modulation, *refs):
    *parts, total_out, out = refs
    total = parts[0][...].astype(F32)
    for p in parts[1:]:
        total = total + p[...].astype(F32)
    total_out[...] = total
    out[...] = modulated_rows(total, modulation)


def summed_modulated(modulation, parts):
    n, d = parts[0].shape
    return pl.pallas_call(
        summed_modulated_kernel,
        out_shape=[shape((n, d), F32), shape((n, d), BF16)],
        in_specs=[VMEM] * (1 + len(parts)),
        out_specs=[VMEM] * 2,
        compiler_params=params(4),
        cost_estimate=NO_COST,
        name="summed_modulated",
    )(modulation, *parts)


def project_kernel(weights, *refs):
    *rows, q_out, k_out, v_out, hidden_out = refs
    rows_now = jnp.concatenate([r[...] for r in rows], axis=0) if len(rows) > 1 else rows[0][...]
    product = jnp.dot(rows_now, weights[...], preferred_element_type=F32)
    queries = product[:, :HD] * SCORE_SCALE
    high = queries.astype(BF16)
    q_out[:, :HD] = high
    q_out[:, HD:] = (queries - high.astype(F32)).astype(BF16)
    k_out[...] = product[:, HD : 2 * HD].astype(BF16)
    v_out[...] = product[:, 2 * HD : 3 * HD].astype(BF16)
    hidden_out[...] = jax.nn.gelu(product[:, 3 * HD :], approximate=True).astype(BF16)


def project(weights, rows):
    n = sum(r.shape[0] for r in rows)
    d, columns = weights.shape
    units = columns - 3 * HD
    return pl.pallas_call(
        project_kernel,
        out_shape=[shape((n, c), BF16) for c in (2 * HD, HD, HD, units)],
        in_specs=[VMEM] * (1 + len(rows)),
        out_specs=[VMEM] * 4,
        compiler_params=params(8),
        cost_estimate=NO_COST,
        name="project",
    )(weights, *rows)


def scores_of(q, keys, bias):
    keys_twice = jnp.concatenate([keys, keys], axis=1)
    return lax.dot_general(q, keys_twice, NT, preferred_element_type=F32) + bias


def weighted(probs, values):
    return jnp.dot(probs, jnp.concatenate([values, jnp.ones_like(values)], axis=1), preferred_element_type=F32)


def stale_kernel(step, q_ref, *refs):
    *sets, top_out, mix_out = refs
    q = q_ref[...]
    n = q.shape[0]
    top = jnp.full((n, 1), NEG, F32)
    mix = jnp.zeros((n, 2 * HD), F32)
    for i in range(0, len(sets), 3):
        keys, values, bias = sets[i : i + 3]
        total = keys.shape[0]
        for j in range(0, total, min(step, total)):
            span = slice(j, j + min(step, total))
            s = scores_of(q, keys[span, :], bias[:, span])
            new_top = jnp.maximum(top, jnp.max(s, axis=1, keepdims=True))
            probs = jnp.exp2(s - new_top).astype(BF16)
            mix = mix * jnp.exp2(top - new_top) + weighted(probs, values[span, :])
            top = new_top
    top_out[...] = jnp.broadcast_to(top, top_out.shape)
    mix_out[...] = mix


def stale_attention(q, sets):
    n = q.shape[0]
    total = sum(s[0].shape[0] for s in sets)
    flat = [a for s in sets for a in s]
    return pl.pallas_call(
        functools.partial(stale_kernel, 512 if n >= 256 else 2048),
        out_shape=[shape((n, HD), F32), shape((n, 2 * HD), F32)],
        in_specs=[VMEM] * (1 + len(flat)),
        out_specs=[VMEM] * 2,
        compiler_params=params(12),
        cost_estimate=NO_COST,
        name="stale",
    )(q, *flat)


def finish_kernel(at, sizes, q, top, mix, hidden, modulation, w_attn, w_mlp, bias, *refs):
    outs = refs[-len(sizes) :]
    count = (len(refs) - len(sizes)) // 2
    keys = jnp.concatenate([r[...] for r in refs[:count]], axis=0)
    values = jnp.concatenate([r[...] for r in refs[count : 2 * count]], axis=0)
    span = slice(at, at + sum(sizes))
    s = scores_of(q[span, :], keys, bias[...])
    old_top = top[span, :1]
    new_top = jnp.maximum(old_top, jnp.max(s, axis=1, keepdims=True))
    probs = jnp.exp2(s - new_top).astype(BF16)
    total = mix[span, :] * jnp.exp2(old_top - new_top) + weighted(probs, values)
    attended = (total[:, :HD] / total[:, HD : HD + 1]).astype(BF16)
    branch = jnp.dot(attended, w_attn[...], preferred_element_type=F32)
    branch = branch + jnp.dot(hidden[span, :], w_mlp[...], preferred_element_type=F32)
    branch = branch * modulation[2:3, :]
    begin = 0
    for n, out in zip(sizes, outs):
        out[...] = branch[begin : begin + n, :].astype(out.dtype)
        begin += n


def finish(at, sizes, dtypes, part, mixed, modulation, w_attn, w_mlp, bias, keys, values):
    d = w_attn.shape[1]
    return pl.pallas_call(
        functools.partial(finish_kernel, at, sizes),
        out_shape=[shape((n, d), t) for n, t in zip(sizes, dtypes)],
        in_specs=[VMEM] * (8 + 2 * len(keys)),
        out_specs=[VMEM] * len(sizes),
        compiler_params=params(8),
        cost_estimate=NO_COST,
        name="finish",
    )(part[0], *mixed, part[3], modulation, w_attn, w_mlp, bias, *keys, *values)


def add_kernel(total, arrived, out):
    out[...] = total[...] + arrived[...].astype(F32)


def add(total, arrived):
    return pl.pallas_call(
        add_kernel,
        out_shape=shape(total.shape, F32),
        in_specs=[VMEM] * 2,
        out_specs=VMEM,
        compiler_params=params(4),
        cost_estimate=pl.CostEstimate(flops=2 * 10**9, bytes_accessed=0, transcendentals=0),
        name="add",
    )(total, arrived)


def split_sum_kernel(current, own, *refs):
    count = own.shape[0] // current.shape[0]
    arrived, outs = refs[:-count], refs[-count:]
    n = current.shape[0]
    for i, out in enumerate(outs):
        span = slice(i * n, (i + 1) * n)
        total = own[span, :]
        for a in arrived:
            total = total + a[span, :].astype(F32)
        if i == 0:
            total = total + current[...].astype(F32)
        out[...] = total.astype(out.dtype)


def split_sum(current, own, arrived, first_dtype):
    n, d = current.shape
    dtypes = [first_dtype] + [BF16] * (own.shape[0] // n - 1)
    return pl.pallas_call(
        split_sum_kernel,
        out_shape=[shape((n, d), t) for t in dtypes],
        in_specs=[VMEM] * (2 + len(arrived)),
        out_specs=[VMEM] * len(dtypes),
        compiler_params=params(4),
        cost_estimate=NO_COST,
        name="split_sum",
    )(current, own, *arrived)


def last_sum_kernel(keep, *refs):
    *arrived, out = refs
    total = arrived[0][...].astype(F32)
    for a in arrived[1:]:
        total = total + a[...].astype(F32)
    out[...] = jnp.where(keep[:, :1] > 0.0, total, 0.0)


def last_sum(keep, parts):
    return pl.pallas_call(
        last_sum_kernel,
        out_shape=shape(parts[0].shape, F32),
        in_specs=[VMEM] * (1 + len(parts)),
        out_specs=VMEM,
        compiler_params=params(4),
        cost_estimate=NO_COST,
        name="last_sum",
    )(keep, *parts)


def on_device(
    sections,
    width,
    activations,
    modulation,
    w_qkv,
    w_mlp_in,
    w_out_attn,
    w_out_mlp,
    key_cache,
    value_cache,
    patch_order,
    patch_lengths,
):
    tok_rows = activations.shape[1]
    mod_rows = modulation[0]
    w_attn = w_out_attn[0]
    w_mlp = w_out_mlp[0]
    keys_all = key_cache[0]
    values_all = value_cache[0]
    others = OFFSETS[1:]

    raw = activations[0]
    raw_near = [raw] + [received(raw, by, 0, sections, width) for by in others]

    spot = jnp.stack([lax.axis_index("section"), lax.axis_index("sp")]).astype(jnp.int32)
    stale0, stale1, fresh0, fresh1, old1, keep = make_masks(
        patch_order, patch_lengths, spot, keys_all.shape[0], tok_rows * width, tok_rows, sections
    )
    weights = side_by_side(jnp.transpose(w_qkv[0], (1, 0, 2)), w_mlp_in[0])
    near = join_modulated(mod_rows, after(raw_near, weights, stale0))
    stale_bias = (stale0, stale1)
    fresh_bias = (fresh0, fresh1)

    old_sets = []
    current = raw
    n = tok_rows * SIDE
    for step in range(TICKS):
        sets = [(keys_all, values_all, stale_bias[step])] + old_sets
        low, high = near
        low_next = received(low, 0, 1, sections, width)
        high_prev = received(high, 0, -1, sections, width)
        high_next = received(high, 0, 1, sections, width)
        low_prev = received(low, 0, -1, sections, width)
        low_far = received(low_next, 0, 1, sections, width)
        high_far = received(high_prev, 0, -1, sections, width)
        part0 = project(weights, [low, high])
        mixed0 = stale_attention(part0[0], sets)
        part1 = project(weights, after([low_next, high_next, low_prev, high_prev], mixed0))
        mixed1 = stale_attention(part1[0], sets)
        part2 = project(weights, after([low_far, high_far], mixed1))
        keys = [part0[1], part1[1], part2[1]]
        values = [part0[2], part1[2], part2[2]]

        def branch_of(sizes, dtype, part, mixed):
            return finish(
                0, sizes, [dtype] * len(sizes), part, mixed, mod_rows, w_attn, w_mlp, fresh_bias[step], keys, values
            )

        out1, out2 = branch_of([n, n], BF16, part1, mixed1)
        back1 = sent(out1, 0, others[0], sections, width)
        back2 = sent(out2, 0, others[1], sections, width)
        mixed2 = stale_attention(after(part2[0], out2), sets)
        (out3,) = branch_of([n], BF16, part2, mixed2)
        back3 = sent(out3, 0, others[2], sections, width)
        (own,) = branch_of([n], F32, after(part0, out3), mixed0)
        total = add(add(own, back1), back2)
        last = step + 1 == TICKS
        pieces = split_sum(current, total, [back3], F32 if last else BF16)
        if last:
            arrived = [sent(p, by, 0, sections, width) for p, by in zip(pieces[1:], others)]
            return last_sum(keep, [pieces[0], *arrived])[None]
        arrived = [sent(p, by, 0, sections, width, 1) for p, by in zip(pieces[1:], others)]
        arrived.append(lax.ppermute(pieces[0], "section", [(i, (i + 1) % sections) for i in range(sections)]))
        current, modulated = summed_modulated(mod_rows, arrived)
        old_sets = list(zip(keys, values, jnp.split(old1, [n, 3 * n], axis=1)))
        near = join([modulated] + [received(modulated, by, 0, sections, width) for by in others])


def solution(mesh):
    placed = (
        P("section", "sp", None),
        P("section", None, None),
        P("section", None, None, "sp"),
        P("section", None, "sp"),
        P("section", "sp", None),
        P("section", "sp", None),
        P("section", None, "sp"),
        P("section", None, "sp"),
        P(),
        P(),
    )
    return jax.shard_map(
        functools.partial(on_device, mesh.shape["section"], mesh.shape["sp"]),
        mesh=mesh,
        in_specs=placed,
        out_specs=P("section", "sp", None),
        check_vma=False,
    )
```
